32 devices in a mesh: dp: 4 (over z), seq: 8 (over y, x, core).
Axes of the slice: x: 2, y: 2, z: 4, core: 2. Of those that a mesh axis runs over, the one named last changes fastest.
Arguments:
- tokens: bfloat16 [4, 16384, 2048], P('dp', 'seq'), may hold values from -6 to 6
- gate: bfloat16 [4, 16384, 2048], P('dp', 'seq'), may hold values from -6 to 6
- cotangent: bfloat16 [4, 16384, 2048], P('dp', 'seq'), may hold values from -6 to 6
- first_factor: bfloat16 [32, 512, 512], P('seq'), may hold values from -0.25 to 0.25
- second_factor: bfloat16 [512, 32, 32], P('seq'), may hold values from -1 to 1
Outputs:
- input_grad: bfloat16 [4, 16384, 2048], P('dp', 'seq')
- gate_grad: bfloat16 [4, 16384, 2048], P('dp', 'seq')
- first_grad: float32 [32, 512, 512], P('seq', 'dp')
- second_grad: float32 [512, 32, 32], P('seq', 'dp')
The draws below stay inside these ranges and needn't reach their ends.
All inputs are finite; a program needn't handle non-finite values.
Results may differ from the reference program's by a relative error of at most 0.0057.
Values may be sent and summed in bfloat16 or wider, within the bound.
No kernel may reach another device: no remote copies, remote signals or barrier semaphores. Data moves between devices by JAX's collectives and lax.ppermute only.
A program may use at most 128 MiB of HBM per device.

```python
import jax
import jax.numpy as jnp
from jax import lax

D = 2048
BS = 512
NB = 32
SEQ_LEN = 16384
BATCH = 4


def block_levels(own_key, dims, split, least, high):
    factor_of, own = 1.0, jax.random.fold_in(own_key, 6)
    for dim, blocks in split:
        steps = jnp.exp(jax.random.uniform(jax.random.fold_in(own, dim), (blocks,), jnp.float32, least / len(split), high / len(split)))
        factor_of = factor_of * jnp.repeat(steps, dims[dim] // blocks).reshape([-1 if axis == dim else 1 for axis in range(len(dims))])
    return factor_of


def normal_values(stream_key, dims, spread, reach, pieces=(), kind=jnp.bfloat16):
    entries = spread * jax.random.normal(stream_key, dims, jnp.float32)
    if pieces:
        entries = entries * block_levels(stream_key, dims, pieces, -0.22, 0.18)
    return jnp.clip(entries, -reach, reach).astype(kind)


def setup_inputs(seed: int = 0) -> dict:
    arg_keys = jax.random.split(jax.random.key(seed), 6)
    tokens = normal_values(arg_keys[0], (BATCH, SEQ_LEN, D), 1.0, 6.0, ((0, 4), (1, 8)))
    gate = normal_values(arg_keys[1], (BATCH, SEQ_LEN, D), 1.0, 6.0, ((0, 4), (1, 8)))
    cotangent = normal_values(arg_keys[2], (BATCH, SEQ_LEN, D), 1.0, 6.0, ((0, 4), (1, 8)))
    first_factor = normal_values(arg_keys[3], (NB, BS, BS), BS ** -0.5, 0.25, ((0, 8),))
    second_factor = normal_values(arg_keys[4], (BS, NB, NB), NB ** -0.5, 1.0, ((0, 8),))
    return dict(tokens=tokens, gate=gate, cotangent=cotangent, first_factor=first_factor, second_factor=second_factor)


def reference(tokens, gate, cotangent, first_factor, second_factor):
    first_wide = first_factor.astype(jnp.float32)
    second_wide = second_factor.astype(jnp.float32)
    highest = lax.Precision.HIGHEST

    def one_sequence(carry, inputs):
        first_acc, second_acc = carry
        seq_in, seq_gate, seq_cot = inputs
        blocks = seq_in.reshape(NB, BS, D).astype(jnp.float32)
        hidden = jnp.einsum('bij,bjc->bic', first_wide, blocks, precision=highest).astype(jnp.bfloat16)
        hidden_wide = hidden.astype(jnp.float32)
        mixed = jnp.einsum('ipb,bic->ipc', second_wide, hidden_wide, precision=highest)
        gate_t = seq_gate.reshape(BS, NB, D).astype(jnp.float32)
        cot_t = seq_cot.reshape(BS, NB, D).astype(jnp.float32)
        gate_grad = (cot_t * mixed).astype(jnp.bfloat16).reshape(SEQ_LEN, D)
        mixed_grad = (cot_t * gate_t).astype(jnp.bfloat16).astype(jnp.float32)
        second_acc = second_acc + jnp.einsum('ipc,bic->ipb', mixed_grad, hidden_wide, precision=highest)
        hidden_grad = jnp.einsum('ipb,ipc->bic', second_wide, mixed_grad, precision=highest).astype(jnp.bfloat16)
        hidden_grad_wide = hidden_grad.astype(jnp.float32)
        first_acc = first_acc + jnp.einsum('bic,bjc->bij', hidden_grad_wide, blocks, precision=highest)
        input_grad = jnp.einsum('bij,bic->bjc', first_wide, hidden_grad_wide, precision=highest)
        input_grad = input_grad.astype(jnp.bfloat16).reshape(SEQ_LEN, D)
        return ((first_acc, second_acc), (input_grad, gate_grad))
    start = (jnp.zeros((NB, BS, BS), jnp.float32), jnp.zeros((BS, NB, NB), jnp.float32))
    (first_acc, second_acc), (input_grad, gate_grad) = lax.scan(one_sequence, start, (tokens, gate, cotangent))
    factor = 1.0 / jnp.sqrt(jnp.float32(D * BATCH))
    return (input_grad, gate_grad, first_acc * factor, second_acc * factor)
```

```python
import functools

import jax
import jax.numpy as jnp
from jax import lax
from jax.experimental import pallas as pl
from jax.experimental.pallas import tpu as pltpu
from jax.sharding import PartitionSpec as P

F32, BF16 = jnp.float32, jnp.bfloat16
G = 8
T = 2 * G
VMEM_LIMIT = 60 * 1024 * 1024
NT = (((1,), (1,)), ((), ()))
ANY = pl.BlockSpec(memory_space=pl.ANY)


def _dot(a, b):
    return jnp.dot(a, b, preferred_element_type=F32)


def _dot_nt(a, b):
    return lax.dot_general(a, b, NT, preferred_element_type=F32)


def _iota(shape, dim):
    return lax.broadcasted_iota(jnp.int32, shape, dim)


def _call(kernel, grid, in_specs, out_specs, out_shape, scratch, flops, nbytes, name, after=(), aliases=None):
    return pl.pallas_call(
        kernel,
        grid_spec=pltpu.PrefetchScalarGridSpec(
            num_scalar_prefetch=1,
            grid=grid,
            in_specs=list(in_specs) + [ANY] * len(after),
            out_specs=out_specs,
            scratch_shapes=scratch,
        ),
        out_shape=out_shape,
        input_output_aliases=aliases or {},
        compiler_params=pltpu.CompilerParams(vmem_limit_bytes=VMEM_LIMIT),
        cost_estimate=pl.CostEstimate(flops=flops, bytes_accessed=nbytes, transcendentals=0),
        name=name,
    )


def _pick(nb, lb, flip):
    block = _iota((nb * G, nb), 0) // G
    block = jnp.bitwise_xor(block // lb, flip) * lb + block % lb
    return (block == _iota((nb * G, nb), 1)).astype(BF16)


def hidden_grad_kernel(nseq, lb, nb, split, me_ref, s_ref, gate_ref, cot_ref, *rest):
    outs, (pick, mask, mt, res) = rest[-4 - (nseq if split else 1):-4], rest[-4:]
    rows, cols = nb * G, G * nb
    width = gate_ref.shape[2]

    @pl.when(pl.program_id(0) == 0)
    def _():
        pick[...] = _pick(nb, lb, me_ref[0] if split else 0)
        same = _iota((rows, cols), 0) % G == _iota((rows, cols), 1) // nb
        mask[...] = same.astype(F32)

    mt[...] = (_dot_nt(pick[...], s_ref[...]) * mask[...]).astype(BF16)
    for c in range(0, width, 256):
        mg = cot_ref[0, :, c:c + 256] * gate_ref[0, :, c:c + 256]
        res[:, c:c + 256] = _dot(mt[...], mg).astype(BF16)
    if split:
        for k in range(nseq):
            outs[k][...] = res[k * lb * G:(k + 1) * lb * G, :].reshape(outs[k].shape)
    else:
        outs[0][...] = res[...].reshape(outs[0].shape)


def hidden_grad(me, s2, gate, cot, after, g0, ng, split, nseq, lb, nb):
    width = gate.shape[2]
    rows = pl.BlockSpec((1, G * nb, width), lambda g, m: (0, g0 + g, 0))
    if split:
        out_specs = [pl.BlockSpec((lb // 2, 1, T, width), lambda g, m: (0, g, 0, 0))] * nseq
        out_shape = [jax.ShapeDtypeStruct((lb // 2, ng, T, width), BF16)] * nseq
    else:
        out_specs = pl.BlockSpec((nseq, lb // 2, 1, T, width), lambda g, m: (0, 0, g, 0, 0))
        out_shape = jax.ShapeDtypeStruct((nseq, lb // 2, ng, T, width), BF16)
    return _call(
        functools.partial(hidden_grad_kernel, nseq, lb, nb, split),
        (ng,),
        [pl.BlockSpec((G * nb, nb), lambda g, m: (g0 + g, 0)), rows, rows],
        out_specs,
        out_shape,
        [
            pltpu.VMEM((nb * G, nb), BF16),
            pltpu.VMEM((nb * G, G * nb), F32),
            pltpu.VMEM((nb * G, G * nb), BF16),
            pltpu.VMEM((nb * G, width), BF16),
        ],
        2 * ng * (G * nb) ** 2 * width,
        6 * ng * G * nb * width,
        "hidden_grad",
        after,
    )(me, s2, gate, cot, *after)


def hidden_kernel(nseq, lo, spans, me_ref, f_ref, x_ref, *rest):
    outs, fp = rest[-1 - nseq * len(spans):-1], rest[-1]
    block = f_ref.shape[1]
    width = x_ref.shape[2]

    @pl.when(pl.program_id(1) == 0)
    def _():
        for b in range(2):
            for k in range(nseq):
                start = pl.multiple_of(jnp.bitwise_xor(me_ref[0], k) * lo, lo)
                fp[b, k * lo:(k + 1) * lo, :] = f_ref[b, pl.ds(start, lo), :]

    both = [
        _dot(fp[b], x_ref[0, b * block:(b + 1) * block, :]).reshape(nseq, lo // G, 1, G, width)
        for b in range(2)
    ]
    res = jnp.concatenate(both, axis=2).reshape(nseq, lo // G, T, width).astype(BF16)
    for j, (g0, ng) in enumerate(spans):
        for k in range(nseq):
            outs[j * nseq + k][0] = res[k, g0:g0 + ng]


def hidden_forward(me, f, x, after, spans, nseq, lo, cb):
    lb, block, _ = f.shape
    width = x.shape[2]
    out_specs, out_shape = [], []
    for _, ng in spans:
        out_specs += [pl.BlockSpec((1, ng, T, cb), lambda b, c, m: (b, 0, 0, c))] * nseq
        out_shape += [jax.ShapeDtypeStruct((lb // 2, ng, T, width), BF16)] * nseq
    outs = _call(
        functools.partial(hidden_kernel, nseq, lo, spans),
        (lb // 2, width // cb),
        [
            pl.BlockSpec((2, block, block), lambda b, c, m: (b, 0, 0)),
            pl.BlockSpec((1, 2 * block, cb), lambda b, c, m: (0, b, c)),
        ],
        out_specs,
        out_shape,
        [pltpu.VMEM((2, block, block), BF16)],
        2 * lb * block * block * width,
        4 * lb * block * width,
        "hidden",
        after,
    )(me, f, x, *after)
    return [list(outs[j * nseq:(j + 1) * nseq]) for j in range(len(spans))]


def block_grads_kernel(nseq, ndp, lo, factor, me_ref, f_ref, x_ref, hg_ref, *rest):
    hgs = dict(zip([0] + _wire_order(nseq), rest[:nseq]))
    dx_ref, kept, sent, ft, grad, acc = rest[-6:]
    c = pl.program_id(1)
    block = f_ref.shape[1]
    width = x_ref.shape[2]

    @pl.when(c == 0)
    def _():
        for b in range(2):
            ft[b] = f_ref[b].T
        acc[...] = jnp.zeros_like(acc)

    def unpack(packed, source, first):
        ng = packed.shape[0]
        wide = packed.astype(F32).reshape(ng, 2, G, width)
        for b in range(2):
            part = wide[:, b].reshape(ng * G, width).astype(BF16)
            grad[b, source, first:first + ng * G, :] = part

    early = hg_ref.shape[2]
    for k in range(nseq):
        unpack(hg_ref[k, 0], k, 0)
        unpack(hgs[k][0], jnp.bitwise_xor(me_ref[0], k), early * G)
    for b in range(2):
        hg = grad[b].reshape(block, width)
        rows = slice(b * block, (b + 1) * block)
        dx_ref[0, rows, :] = _dot(ft[b], hg).astype(BF16)
        acc[b] += _dot_nt(hg, x_ref[0, rows, :])

    @pl.when(c == pl.num_programs(1) - 1)
    def _():
        share = block // ndp
        for slot in range(ndp):
            start = pl.multiple_of(jnp.bitwise_xor(me_ref[1], slot) * share, share)
            part = acc[:, pl.ds(start, share), :] * factor
            to = sent if slot % 2 else kept
            to[slot // 2] = part.astype(to.dtype)


def block_grads(me, f, x, hg, hgs, after, nseq, ndp, factor, cb):
    lb, block, _ = f.shape
    width = x.shape[2]
    share = block // ndp
    lo = block // nseq
    rows = pl.BlockSpec((1, 2 * block, cb), lambda b, c, m: (0, b, c))
    return _call(
        functools.partial(block_grads_kernel, nseq, ndp, lo, factor),
        (lb // 2, width // cb),
        [
            pl.BlockSpec((2, block, block), lambda b, c, m: (b, 0, 0)),
            rows,
            pl.BlockSpec((nseq, 1, hg.shape[2], T, cb), lambda b, c, m: (0, b, 0, 0, c)),
        ]
        + [pl.BlockSpec((1, hgs[0].shape[1], T, cb), lambda b, c, m: (b, 0, 0, c))] * nseq,
        [rows] + [pl.BlockSpec((ndp // 2, 2, share, block), lambda b, c, m: (0, b, 0, 0))] * 2,
        [
            jax.ShapeDtypeStruct(x.shape, BF16),
            jax.ShapeDtypeStruct((ndp // 2, lb, share, block), F32),
            jax.ShapeDtypeStruct((ndp // 2, lb, share, block), BF16),
        ],
        [
            pltpu.VMEM((2, block, block), BF16),
            pltpu.VMEM((2, nseq, lo, cb), BF16),
            pltpu.VMEM((2, block, block), F32),
        ],
        4 * lb * block * block * width,
        6 * lb * block * width,
        "block_grads",
        after,
    )(me, f, x, hg, *[hgs[k] for k in [0] + _wire_order(nseq)], *after)


def mixed_kernel(nseq, ndp, lb, nb, factor, me_ref, s_ref, gate_ref, cot_ref, *rest):
    hs = dict(zip([0] + _wire_order(nseq), rest[:nseq]))
    gg_ref, out, pick, mask, order, choose, m, hid, mg = rest[-9:]
    rows, cols = nb * G, G * nb
    share = nb // ndp
    width = gg_ref.shape[2]

    @pl.when(pl.program_id(0) == 0)
    def _():
        pick[...] = _pick(nb, lb, me_ref[0])
        same = _iota((cols, rows), 1) % G == _iota((cols, rows), 0) // nb
        mask[...] = same.astype(F32)
        r = _iota((nb, nb), 1)
        block = jnp.bitwise_xor(r // lb, me_ref[0]) * lb + r % lb
        order[...] = (block == _iota((nb, nb), 0)).astype(BF16)
        q = _iota((cols, cols), 1)
        choose[...] = (_iota((cols, cols), 0) == (q % G) * nb + q // G).astype(BF16)

    m[...] = (_dot_nt(s_ref[...], pick[...]) * mask[...]).astype(BF16)
    for k in range(nseq):
        hid[k * lb * G:(k + 1) * lb * G, :] = hs[k][...].reshape(lb * G, width)
    for c in range(0, width, 256):
        cot = cot_ref[0, :, c:c + 256]
        mixed = _dot(m[...], hid[:, c:c + 256])
        gg_ref[0, :, c:c + 256] = (cot.astype(F32) * mixed).astype(BF16)
        mg[:, c:c + 256] = cot * gate_ref[0, :, c:c + 256]
    kept = _dot_nt(mg[...], hid[...]) * mask[...]
    terms = jnp.sum(kept.T.reshape(nb, G, cols), axis=1) * factor
    terms = _dot(order[...], terms.astype(BF16)).astype(BF16)
    terms = _dot(terms, choose[...])
    tall = out.shape[2]
    for z in range(ndp):
        part = terms[:, z * share * G:(z + 1) * share * G]
        part = [part[r:r + tall] for r in range(0, nb, tall)]
        out[z, 0] = jnp.concatenate(part, axis=1).astype(BF16)


def mixed_stage(me, s2, gate, cot, hs, prev, after, g0, ng, groups, nseq, ndp, lb, nb, factor):
    width = gate.shape[2]
    rows = pl.BlockSpec((1, G * nb, width), lambda g, m: (0, g0 + g, 0))
    share = nb // ndp
    extra = list(prev) + list(after)
    square = (G * nb, nb * G)
    wide = max(128, share * G)
    tall = nb * share * G // wide
    return _call(
        functools.partial(mixed_kernel, nseq, ndp, lb, nb, factor),
        (ng,),
        [pl.BlockSpec((G * nb, nb), lambda g, m: (g0 + g, 0)), rows, rows]
        + [pl.BlockSpec((lb // 2, 1, T, width), lambda g, m: (0, g, 0, 0))] * nseq,
        [rows, pl.BlockSpec((ndp, 1, tall, wide), lambda g, m: (0, g0 + g, 0, 0))],
        [
            jax.ShapeDtypeStruct(gate.shape, BF16),
            jax.ShapeDtypeStruct((ndp, groups, tall, wide), BF16),
        ],
        [
            pltpu.VMEM((nb * G, nb), BF16),
            pltpu.VMEM(square, F32),
            pltpu.VMEM((nb, nb), BF16),
            pltpu.VMEM((G * nb, G * nb), BF16),
            pltpu.VMEM(square, BF16),
            pltpu.VMEM((nb * G, width), BF16),
            pltpu.VMEM((G * nb, width), BF16),
        ],
        4 * ng * (G * nb) ** 2 * width,
        8 * ng * G * nb * width,
        "mixed",
        extra,
        {4 + nseq + i: i for i in range(len(prev))},
    )(me, s2, gate, cot, *[hs[k] for k in [0] + _wire_order(nseq)], *extra)


def _wire_order(size):
    ks = list(range(2, size))
    last = [k for k in ks if k % 2]
    return [k for k in ks if k % 2 == 0][::-1] + last[::-1] + [1]


def _swap(parts, axis, size, differences):
    got = dict([(0, parts[0])])
    for k in differences:
        got[k] = lax.ppermute(parts[k], axis, [(s, s ^ k) for s in range(size)])
    return got


def _halve(kept, sent, axis, size):
    step = 1
    while True:
        got = lax.ppermute(sent, axis, [(z, z ^ step) for z in range(size)])
        kept = kept + got.astype(F32)
        step *= 2
        if step == size:
            return kept[0]
        kept, sent = kept[0::2], kept[1::2].astype(BF16)


def _behind(parts, ahead, count):
    first = _wire_order(len(ahead))[:count]
    parts, arrived = lax.optimization_barrier((parts, [ahead[k] for k in first]))
    for k, part in zip(first, arrived):
        ahead[k] = part
    return parts


def _exchange(parts, axis):
    return lax.all_to_all(parts, axis, split_axis=0, concat_axis=0, tiled=True)


def _total(parts):
    return jnp.sum(parts.astype(F32), axis=0)


def local(tokens, gate, cotangent, first_factor, second_factor):
    seqs, _, width = tokens.shape
    ndp, nseq = lax.axis_size("dp"), lax.axis_size("seq")
    lb = first_factor.shape[0]
    lo, nb = second_factor.shape[:2]
    groups = lo // G
    early = groups // 4 if groups >= 8 else groups // 2
    late = early
    factor = 1.0 / float(width * seqs * ndp) ** 0.5
    me = jnp.stack([lax.axis_index("seq"), lax.axis_index("dp")]).astype(jnp.int32)

    s2_early = second_factor[:early * G].reshape(early * G * nb, nb)
    still = jnp.zeros_like(me)
    back_a = hidden_grad(still, s2_early, gate, cotangent, (), 0, early, False, nseq, lb, nb)
    second_factor, back_a = lax.optimization_barrier((second_factor, back_a))
    s2 = second_factor.reshape(lo * nb, nb)
    grad_a = lax.all_to_all(back_a, "seq", split_axis=0, concat_axis=0, tiled=True)
    back_b = hidden_grad(
        me, s2, gate, cotangent, (back_a,), early, groups - early, True, nseq, lb, nb
    )
    spans = ((0, groups - late), (groups - late, late))
    hidden_b, hidden_c = hidden_forward(
        me, first_factor, tokens, (back_b[0],), spans, nseq, lo, 1024
    )
    back_b, grad_a, hidden_b = lax.optimization_barrier((back_b, grad_a, hidden_b))
    grad_b = _swap(back_b, "seq", nseq, _wire_order(nseq))
    wire = _wire_order(nseq)
    got_b = _swap(_behind(hidden_b, grad_b, nseq - 3), "seq", nseq, wire)
    got_c = _swap(_behind(hidden_c, got_b, 3), "seq", nseq, wire)
    input_grad, kept, sent = block_grads(
        me, first_factor, tokens, grad_a, grad_b, (), nseq, ndp, factor, 1024
    )
    sent = _behind(sent, got_b, 2)

    first_share = _halve(kept, sent, "dp", ndp)

    gate_grad, terms = mixed_stage(
        me, s2, gate, cotangent, got_b, (), (sent,), 0, groups - late, groups,
        nseq, ndp, lb, nb, factor
    )
    gate_grad, terms = mixed_stage(
        me, s2, gate, cotangent, got_c, (gate_grad, terms), (), groups - late, late, groups,
        nseq, ndp, lb, nb, factor
    )
    share = nb // ndp
    second_share = _total(_exchange(terms, "dp")).reshape(groups, terms.shape[2], -1, share, G)
    second_share = second_share.transpose(0, 4, 3, 2, 1).reshape(lo, share, nb)
    return (input_grad, gate_grad, first_share, second_share)


def solution(mesh):
    placed = (
        P("dp", "seq", None),
        P("dp", "seq", None),
        P("dp", "seq", None),
        P("seq", None, None),
        P("seq", None, None),
    )
    return jax.shard_map(
        local,
        mesh=mesh,
        in_specs=placed,
        out_specs=(
            P("dp", "seq", None),
            P("dp", "seq", None),
            P("seq", "dp", None),
            P("seq", "dp", None),
        ),
        check_vma=False,
    )
```

```python
import functools

import jax
import jax.numpy as jnp
import numpy as np
from jax import lax
from jax.experimental import pallas as pl
from jax.experimental.pallas import tpu as pltpu
from jax.sharding import PartitionSpec as P

F32, BF16 = jnp.float32, jnp.bfloat16
G = 8
T = 2 * G
VMEM_LIMIT = 60 * 1024 * 1024
NT = (((1,), (1,)), ((), ()))
ANY = pl.BlockSpec(memory_space=pl.ANY)


def _dot(a, b):
    return jnp.dot(a, b, preferred_element_type=F32)


def _dot_nt(a, b):
    return lax.dot_general(a, b, NT, preferred_element_type=F32)


def _iota(shape, dim):
    return lax.broadcasted_iota(jnp.int32, shape, dim)


def _call(kernel, grid, in_specs, out_specs, out_shape, scratch, flops, nbytes, name, after=(), aliases=None):
    return pl.pallas_call(
        kernel,
        grid_spec=pltpu.PrefetchScalarGridSpec(
            num_scalar_prefetch=1,
            grid=grid,
            in_specs=list(in_specs) + [ANY] * len(after),
            out_specs=out_specs,
            scratch_shapes=scratch,
        ),
        out_shape=out_shape,
        input_output_aliases=aliases or {},
        compiler_params=pltpu.CompilerParams(vmem_limit_bytes=VMEM_LIMIT),
        cost_estimate=pl.CostEstimate(flops=flops, bytes_accessed=nbytes, transcendentals=0),
        name=name,
    )


def _pick(nb, lb, flip):
    block = _iota((nb * G, nb), 0) // G
    block = jnp.bitwise_xor(block // lb, flip) * lb + block % lb
    return (block == _iota((nb * G, nb), 1)).astype(BF16)


def hidden_grad_kernel(nseq, lb, nb, split, me_ref, s_ref, gate_ref, cot_ref, *rest):
    outs, (pick, mask, mt, res) = rest[-4 - (nseq if split else 1):-4], rest[-4:]
    rows, cols = nb * G, G * nb
    width = gate_ref.shape[2]

    @pl.when(pl.program_id(0) == 0)
    def _():
        pick[...] = _pick(nb, lb, me_ref[0] if split else 0)
        same = _iota((rows, cols), 0) % G == _iota((rows, cols), 1) // nb
        mask[...] = same.astype(F32)

    mt[...] = (_dot_nt(pick[...], s_ref[...]) * mask[...]).astype(BF16)
    for c in range(0, width, 256):
        mg = cot_ref[0, :, c:c + 256] * gate_ref[0, :, c:c + 256]
        res[:, c:c + 256] = _dot(mt[...], mg).astype(BF16)
    if split:
        for k in range(nseq):
            outs[k][...] = res[k * lb * G:(k + 1) * lb * G, :].reshape(outs[k].shape)
    else:
        outs[0][...] = res[...].reshape(outs[0].shape)


def hidden_grad(me, s2, gate, cot, after, g0, ng, split, nseq, lb, nb):
    width = gate.shape[2]
    rows = pl.BlockSpec((1, G * nb, width), lambda g, m: (0, g0 + g, 0))
    if split:
        out_specs = [pl.BlockSpec((lb // 2, 1, T, width), lambda g, m: (0, g, 0, 0))] * nseq
        out_shape = [jax.ShapeDtypeStruct((lb // 2, ng, T, width), BF16)] * nseq
    else:
        out_specs = pl.BlockSpec((nseq, lb // 2, 1, T, width), lambda g, m: (0, 0, g, 0, 0))
        out_shape = jax.ShapeDtypeStruct((nseq, lb // 2, ng, T, width), BF16)
    return _call(
        functools.partial(hidden_grad_kernel, nseq, lb, nb, split),
        (ng,),
        [pl.BlockSpec((G * nb, nb), lambda g, m: (g0 + g, 0)), rows, rows],
        out_specs,
        out_shape,
        [
            pltpu.VMEM((nb * G, nb), BF16),
            pltpu.VMEM((nb * G, G * nb), F32),
            pltpu.VMEM((nb * G, G * nb), BF16),
            pltpu.VMEM((nb * G, width), BF16),
        ],
        2 * ng * (G * nb) ** 2 * width,
        6 * ng * G * nb * width,
        "hidden_grad",
        after,
    )(me, s2, gate, cot, *after)


def hidden_kernel(nseq, lo, spans, me_ref, f_ref, x_ref, *rest):
    outs, fp = rest[-1 - nseq * len(spans):-1], rest[-1]
    block = f_ref.shape[1]
    width = x_ref.shape[2]

    @pl.when(pl.program_id(1) == 0)
    def _():
        for b in range(2):
            for k in range(nseq):
                start = pl.multiple_of(jnp.bitwise_xor(me_ref[0], k) * lo, lo)
                fp[b, k * lo:(k + 1) * lo, :] = f_ref[b, pl.ds(start, lo), :]

    both = [
        _dot(fp[b], x_ref[0, b * block:(b + 1) * block, :]).reshape(nseq, lo // G, 1, G, width)
        for b in range(2)
    ]
    res = jnp.concatenate(both, axis=2).reshape(nseq, lo // G, T, width).astype(BF16)
    for j, (g0, ng) in enumerate(spans):
        for k in range(nseq):
            outs[j * nseq + k][0] = res[k, g0:g0 + ng]


def hidden_forward(me, f, x, after, spans, nseq, lo, cb):
    lb, block, _ = f.shape
    width = x.shape[2]
    out_specs, out_shape = [], []
    for _, ng in spans:
        out_specs += [pl.BlockSpec((1, ng, T, cb), lambda b, c, m: (b, 0, 0, c))] * nseq
        out_shape += [jax.ShapeDtypeStruct((lb // 2, ng, T, width), BF16)] * nseq
    outs = _call(
        functools.partial(hidden_kernel, nseq, lo, spans),
        (lb // 2, width // cb),
        [
            pl.BlockSpec((2, block, block), lambda b, c, m: (b, 0, 0)),
            pl.BlockSpec((1, 2 * block, cb), lambda b, c, m: (0, b, c)),
        ],
        out_specs,
        out_shape,
        [pltpu.VMEM((2, block, block), BF16)],
        2 * lb * block * block * width,
        4 * lb * block * width,
        "hidden",
        after,
    )(me, f, x, *after)
    return [list(outs[j * nseq:(j + 1) * nseq]) for j in range(len(spans))]


def block_grads_kernel(nseq, ndp, lo, factor, me_ref, f_ref, x_ref, hg_ref, *rest):
    hgs = dict(zip([0] + _wire_order(nseq), rest[:nseq]))
    dx_ref, kept, sent, ft, grad, acc = rest[-6:]
    c = pl.program_id(1)
    block = f_ref.shape[1]
    width = x_ref.shape[2]

    @pl.when(c == 0)
    def _():
        for b in range(2):
            ft[b] = f_ref[b].T
        acc[...] = jnp.zeros_like(acc)

    def unpack(packed, source, first):
        ng = packed.shape[0]
        wide = packed.astype(F32).reshape(ng, 2, G, width)
        for b in range(2):
            part = wide[:, b].reshape(ng * G, width).astype(BF16)
            grad[b, source, first:first + ng * G, :] = part

    early = hg_ref.shape[2]
    for k in range(nseq):
        unpack(hg_ref[k, 0], k, 0)
        unpack(hgs[k][0], jnp.bitwise_xor(me_ref[0], k), early * G)
    for b in range(2):
        hg = grad[b].reshape(block, width)
        rows = slice(b * block, (b + 1) * block)
        dx_ref[0, rows, :] = _dot(ft[b], hg).astype(BF16)
        acc[b] += _dot_nt(hg, x_ref[0, rows, :])

    @pl.when(c == pl.num_programs(1) - 1)
    def _():
        share = block // ndp
        for slot in range(ndp):
            start = pl.multiple_of(jnp.bitwise_xor(me_ref[1], slot) * share, share)
            part = acc[:, pl.ds(start, share), :] * factor
            to = sent if slot % 2 else kept
            to[slot // 2] = part.astype(to.dtype)


def block_grads(me, f, x, hg, hgs, after, nseq, ndp, factor, cb):
    lb, block, _ = f.shape
    width = x.shape[2]
    share = block // ndp
    lo = block // nseq
    rows = pl.BlockSpec((1, 2 * block, cb), lambda b, c, m: (0, b, c))
    return _call(
        functools.partial(block_grads_kernel, nseq, ndp, lo, factor),
        (lb // 2, width // cb),
        [
            pl.BlockSpec((2, block, block), lambda b, c, m: (b, 0, 0)),
            rows,
            pl.BlockSpec((nseq, 1, hg.shape[2], T, cb), lambda b, c, m: (0, b, 0, 0, c)),
        ]
        + [pl.BlockSpec((1, hgs[0].shape[1], T, cb), lambda b, c, m: (b, 0, 0, c))] * nseq,
        [rows] + [pl.BlockSpec((ndp // 2, 2, share, block), lambda b, c, m: (0, b, 0, 0))] * 2,
        [
            jax.ShapeDtypeStruct(x.shape, BF16),
            jax.ShapeDtypeStruct((ndp // 2, lb, share, block), F32),
            jax.ShapeDtypeStruct((ndp // 2, lb, share, block), BF16),
        ],
        [
            pltpu.VMEM((2, block, block), BF16),
            pltpu.VMEM((2, nseq, lo, cb), BF16),
            pltpu.VMEM((2, block, block), F32),
        ],
        4 * lb * block * block * width,
        6 * lb * block * width,
        "block_grads",
        after,
    )(me, f, x, hg, *[hgs[k] for k in [0] + _wire_order(nseq)], *after)


def mixed_kernel(nseq, ndp, lb, nb, factor, me_ref, s_ref, gate_ref, cot_ref, *rest):
    hs = dict(zip([0] + _wire_order(nseq), rest[:nseq]))
    gg_ref, out, pick, mask, order, choose, m, hid, mg = rest[-9:]
    rows, cols = nb * G, G * nb
    share = nb // ndp
    width = gg_ref.shape[2]

    @pl.when(pl.program_id(0) == 0)
    def _():
        pick[...] = _pick(nb, lb, me_ref[0])
        same = _iota((cols, rows), 1) % G == _iota((cols, rows), 0) // nb
        mask[...] = same.astype(F32)
        r = _iota((nb, nb), 1)
        block = jnp.bitwise_xor(r // lb, me_ref[0]) * lb + r % lb
        order[...] = (block == _iota((nb, nb), 0)).astype(BF16)
        q = _iota((cols, cols), 1)
        choose[...] = (_iota((cols, cols), 0) == (q % G) * nb + q // G).astype(BF16)

    m[...] = (_dot_nt(s_ref[...], pick[...]) * mask[...]).astype(BF16)
    for k in range(nseq):
        hid[k * lb * G:(k + 1) * lb * G, :] = hs[k][...].reshape(lb * G, width)
    for c in range(0, width, 256):
        cot = cot_ref[0, :, c:c + 256]
        mixed = _dot(m[...], hid[:, c:c + 256])
        gg_ref[0, :, c:c + 256] = (cot.astype(F32) * mixed).astype(BF16)
        mg[:, c:c + 256] = cot * gate_ref[0, :, c:c + 256]
    kept = _dot_nt(mg[...], hid[...]) * mask[...]
    terms = jnp.sum(kept.T.reshape(nb, G, cols), axis=1) * factor
    terms = _dot(order[...], terms.astype(BF16)).astype(BF16)
    terms = _dot(terms, choose[...])
    tall = out.shape[2]
    for z in range(ndp):
        part = terms[:, z * share * G:(z + 1) * share * G]
        part = [part[r:r + tall] for r in range(0, nb, tall)]
        out[z, 0] = jnp.concatenate(part, axis=1).astype(BF16)


def mixed_stage(me, s2, gate, cot, hs, prev, after, g0, ng, groups, nseq, ndp, lb, nb, factor):
    width = gate.shape[2]
    rows = pl.BlockSpec((1, G * nb, width), lambda g, m: (0, g0 + g, 0))
    share = nb // ndp
    extra = list(prev) + list(after)
    square = (G * nb, nb * G)
    wide = max(128, share * G)
    tall = nb * share * G // wide
    return _call(
        functools.partial(mixed_kernel, nseq, ndp, lb, nb, factor),
        (ng,),
        [pl.BlockSpec((G * nb, nb), lambda g, m: (g0 + g, 0)), rows, rows]
        + [pl.BlockSpec((lb // 2, 1, T, width), lambda g, m: (0, g, 0, 0))] * nseq,
        [rows, pl.BlockSpec((ndp, 1, tall, wide), lambda g, m: (0, g0 + g, 0, 0))],
        [
            jax.ShapeDtypeStruct(gate.shape, BF16),
            jax.ShapeDtypeStruct((ndp, groups, tall, wide), BF16),
        ],
        [
            pltpu.VMEM((nb * G, nb), BF16),
            pltpu.VMEM(square, F32),
            pltpu.VMEM((nb, nb), BF16),
            pltpu.VMEM((G * nb, G * nb), BF16),
            pltpu.VMEM(square, BF16),
            pltpu.VMEM((nb * G, width), BF16),
            pltpu.VMEM((G * nb, width), BF16),
        ],
        4 * ng * (G * nb) ** 2 * width,
        8 * ng * G * nb * width,
        "mixed",
        extra,
        {4 + nseq + i: i for i in range(len(prev))},
    )(me, s2, gate, cot, *[hs[k] for k in [0] + _wire_order(nseq)], *extra)


def _wire_order(size):
    ks = list(range(2, size))
    last = [k for k in ks if k % 2]
    return [k for k in ks if k % 2 == 0][::-1] + last[::-1] + [1]


def _swap(parts, axis, size, differences):
    got = dict([(0, parts[0])])
    for k in differences:
        got[k] = lax.ppermute(parts[k], axis, [(s, s ^ k) for s in range(size)])
    return got


def _pass(part, axis, size, step):
    return lax.ppermute(part, axis, [(z, z ^ step) for z in range(size)])


def _halve(kept, got, axis, size):
    step = 2
    while step < size:
        kept = kept + got.astype(F32)
        got = _pass(kept[1::2].astype(BF16), axis, size, step)
        kept = kept[0::2]
        step *= 2
    return kept, got


def _behind(parts, ahead, count):
    first = _wire_order(len(ahead))[:count]
    parts, arrived = lax.optimization_barrier((parts, [ahead[k] for k in first]))
    for k, part in zip(first, arrived):
        ahead[k] = part
    return parts


def _exchange(parts, axis):
    return lax.all_to_all(parts, axis, split_axis=0, concat_axis=0, tiled=True)


def _total(parts):
    return jnp.sum(parts.astype(F32), axis=0)


def local(tokens, gate, cotangent, first_factor, second_factor):
    seqs, _, width = tokens.shape
    ndp, nseq = lax.axis_size("dp"), lax.axis_size("seq")
    lb = first_factor.shape[0]
    lo, nb = second_factor.shape[:2]
    groups = lo // G
    early = groups // 4 if groups >= 8 else groups // 2
    late = early
    factor = 1.0 / float(width * seqs * ndp) ** 0.5
    me = jnp.stack([lax.axis_index("seq"), lax.axis_index("dp")]).astype(jnp.int32)

    s2_early = second_factor[:early * G].reshape(early * G * nb, nb)
    still = np.array([0, 1], np.int32)
    back_a = hidden_grad(still, s2_early, gate, cotangent, (), 0, early, False, nseq, lb, nb)
    second_factor, back_a = lax.optimization_barrier((second_factor, back_a))
    s2 = second_factor.reshape(lo * nb, nb)
    grad_a = lax.all_to_all(back_a, "seq", split_axis=0, concat_axis=0, tiled=True)
    back_b = hidden_grad(
        me, s2, gate, cotangent, (back_a,), early, groups - early, True, nseq, lb, nb
    )
    spans = ((0, groups - late), (groups - late, late))
    hidden_b, hidden_c = hidden_forward(
        me, first_factor, tokens, (back_b[0],), spans, nseq, lo, 1024
    )
    back_b, grad_a, hidden_b = lax.optimization_barrier((back_b, grad_a, hidden_b))
    grad_b = _swap(back_b, "seq", nseq, _wire_order(nseq))
    wire = _wire_order(nseq)
    got_b = _swap(_behind(hidden_b, grad_b, nseq - 3), "seq", nseq, wire)
    hidden_c = _behind(hidden_c, got_b, 3)
    got_c = _swap(hidden_c, "seq", nseq, wire[:-1])
    input_grad, kept, sent = block_grads(
        me, first_factor, tokens, grad_a, grad_b, (), nseq, ndp, factor, 1024
    )
    sent = _behind(sent, got_b, 2)

    halves = _pass(sent, "dp", ndp, 1)

    gate_grad, terms = mixed_stage(
        me, s2, gate, cotangent, got_b, (), (sent,), 0, groups - late, groups,
        nseq, ndp, lb, nb, factor
    )
    last_c, terms = lax.optimization_barrier((hidden_c[wire[-1]], terms))
    hidden_c[wire[-1]] = last_c
    got_c.update(_swap(hidden_c, "seq", nseq, wire[-1:]))
    kept, first_got = _halve(kept, halves, "dp", ndp)
    gate_grad, terms = mixed_stage(
        me, s2, gate, cotangent, got_c, (gate_grad, terms), (), groups - late, late, groups,
        nseq, ndp, lb, nb, factor
    )
    share = nb // ndp
    terms, first_got = lax.optimization_barrier((terms, first_got))
    first_share = (kept + first_got.astype(F32))[0]
    second_share = _total(_exchange(terms, "dp")).reshape(groups, terms.shape[2], -1, share, G)
    second_share = second_share.transpose(0, 4, 3, 2, 1).reshape(lo, share, nb)
    return (input_grad, gate_grad, first_share, second_share)


def solution(mesh):
    placed = (
        P("dp", "seq", None),
        P("dp", "seq", None),
        P("dp", "seq", None),
        P("seq", None, None),
        P("seq", None, None),
    )
    return jax.shard_map(
        local,
        mesh=mesh,
        in_specs=placed,
        out_specs=(
            P("dp", "seq", None),
            P("dp", "seq", None),
            P("seq", "dp", None),
            P("seq", "dp", None),
        ),
        check_vma=False,
    )
```

```python
import functools

import jax
import jax.numpy as jnp
import numpy as np
from jax import lax
from jax.experimental import pallas as pl
from jax.experimental.pallas import tpu as pltpu
from jax.sharding import PartitionSpec as P

F32, BF16 = jnp.float32, jnp.bfloat16
G = 8
T = 2 * G
VMEM_LIMIT = 60 * 1024 * 1024
NT = (((1,), (1,)), ((), ()))
ANY = pl.BlockSpec(memory_space=pl.ANY)


def _dot(a, b):
    return jnp.dot(a, b, preferred_element_type=F32)


def _dot_nt(a, b):
    return lax.dot_general(a, b, NT, preferred_element_type=F32)


def _iota(shape, dim):
    return lax.broadcasted_iota(jnp.int32, shape, dim)


def _call(kernel, grid, in_specs, out_specs, out_shape, scratch, flops, nbytes, name, after=(), aliases=None):
    return pl.pallas_call(
        kernel,
        grid_spec=pltpu.PrefetchScalarGridSpec(
            num_scalar_prefetch=1,
            grid=grid,
            in_specs=list(in_specs) + [ANY] * len(after),
            out_specs=out_specs,
            scratch_shapes=scratch,
        ),
        out_shape=out_shape,
        input_output_aliases=aliases or {},
        compiler_params=pltpu.CompilerParams(vmem_limit_bytes=VMEM_LIMIT),
        cost_estimate=pl.CostEstimate(flops=flops, bytes_accessed=nbytes, transcendentals=0),
        name=name,
    )


def _pick(nb, lb, flip):
    block = _iota((nb * G, nb), 0) // G
    block = jnp.bitwise_xor(block // lb, flip) * lb + block % lb
    return (block == _iota((nb * G, nb), 1)).astype(BF16)


def hidden_grad_kernel(nseq, lb, nb, split, me_ref, s_ref, gate_ref, cot_ref, *rest):
    outs, (pick, mask, mt, res) = rest[-4 - (nseq if split else 1):-4], rest[-4:]
    rows, cols = nb * G, G * nb
    width = gate_ref.shape[2]

    @pl.when(pl.program_id(0) == 0)
    def _():
        pick[...] = _pick(nb, lb, me_ref[0] if split else 0)
        same = _iota((rows, cols), 0) % G == _iota((rows, cols), 1) // nb
        mask[...] = same.astype(F32)

    mt[...] = (_dot_nt(pick[...], s_ref[...]) * mask[...]).astype(BF16)
    for c in range(0, width, 256):
        mg = cot_ref[0, :, c:c + 256] * gate_ref[0, :, c:c + 256]
        res[:, c:c + 256] = _dot(mt[...], mg).astype(BF16)
    if split:
        for k in range(nseq):
            outs[k][...] = res[k * lb * G:(k + 1) * lb * G, :].reshape(outs[k].shape)
    else:
        outs[0][...] = res[...].reshape(outs[0].shape)


def hidden_grad(me, s2, gate, cot, after, g0, ng, split, nseq, lb, nb):
    width = gate.shape[2]
    rows = pl.BlockSpec((1, G * nb, width), lambda g, m: (0, g0 + g, 0))
    if split:
        out_specs = [pl.BlockSpec((lb // 2, 1, T, width), lambda g, m: (0, g, 0, 0))] * nseq
        out_shape = [jax.ShapeDtypeStruct((lb // 2, ng, T, width), BF16)] * nseq
    else:
        out_specs = pl.BlockSpec((nseq, lb // 2, 1, T, width), lambda g, m: (0, 0, g, 0, 0))
        out_shape = jax.ShapeDtypeStruct((nseq, lb // 2, ng, T, width), BF16)
    return _call(
        functools.partial(hidden_grad_kernel, nseq, lb, nb, split),
        (ng,),
        [pl.BlockSpec((G * nb, nb), lambda g, m: (g0 + g, 0)), rows, rows],
        out_specs,
        out_shape,
        [
            pltpu.VMEM((nb * G, nb), BF16),
            pltpu.VMEM((nb * G, G * nb), F32),
            pltpu.VMEM((nb * G, G * nb), BF16),
            pltpu.VMEM((nb * G, width), BF16),
        ],
        2 * ng * (G * nb) ** 2 * width,
        6 * ng * G * nb * width,
        "hidden_grad",
        after,
    )(me, s2, gate, cot, *after)


def hidden_kernel(nseq, lo, spans, me_ref, f_ref, x_ref, *rest):
    outs, fp = rest[-1 - nseq * len(spans):-1], rest[-1]
    block = f_ref.shape[1]
    width = x_ref.shape[2]

    @pl.when(pl.program_id(1) == 0)
    def _():
        for b in range(2):
            for k in range(nseq):
                start = pl.multiple_of(jnp.bitwise_xor(me_ref[0], k) * lo, lo)
                fp[b, k * lo:(k + 1) * lo, :] = f_ref[b, pl.ds(start, lo), :]

    both = [
        _dot(fp[b], x_ref[0, b * block:(b + 1) * block, :]).reshape(nseq, lo // G, 1, G, width)
        for b in range(2)
    ]
    res = jnp.concatenate(both, axis=2).reshape(nseq, lo // G, T, width).astype(BF16)
    for j, (g0, ng) in enumerate(spans):
        for k in range(nseq):
            outs[j * nseq + k][0] = res[k, g0:g0 + ng]


def hidden_forward(me, f, x, after, spans, nseq, lo, cb):
    lb, block, _ = f.shape
    width = x.shape[2]
    out_specs, out_shape = [], []
    for _, ng in spans:
        out_specs += [pl.BlockSpec((1, ng, T, cb), lambda b, c, m: (b, 0, 0, c))] * nseq
        out_shape += [jax.ShapeDtypeStruct((lb // 2, ng, T, width), BF16)] * nseq
    outs = _call(
        functools.partial(hidden_kernel, nseq, lo, spans),
        (lb // 2, width // cb),
        [
            pl.BlockSpec((2, block, block), lambda b, c, m: (b, 0, 0)),
            pl.BlockSpec((1, 2 * block, cb), lambda b, c, m: (0, b, c)),
        ],
        out_specs,
        out_shape,
        [pltpu.VMEM((2, block, block), BF16)],
        2 * lb * block * block * width,
        4 * lb * block * width,
        "hidden",
        after,
    )(me, f, x, *after)
    return [list(outs[j * nseq:(j + 1) * nseq]) for j in range(len(spans))]


def block_grads_kernel(nseq, ndp, lo, factor, me_ref, f_ref, x_ref, hg_ref, *rest):
    hgs = dict(zip([0] + _wire_order(nseq), rest[:nseq]))
    dx_ref, kept, sent, ft, grad, acc = rest[-6:]
    c = pl.program_id(1)
    block = f_ref.shape[1]
    width = x_ref.shape[2]

    @pl.when(c == 0)
    def _():
        for b in range(2):
            ft[b] = f_ref[b].T
        acc[...] = jnp.zeros_like(acc)

    def unpack(packed, source, first):
        ng = packed.shape[0]
        wide = packed.astype(F32).reshape(ng, 2, G, width)
        for b in range(2):
            part = wide[:, b].reshape(ng * G, width).astype(BF16)
            grad[b, source, first:first + ng * G, :] = part

    early = hg_ref.shape[2]
    for k in range(nseq):
        unpack(hg_ref[k, 0], k, 0)
        unpack(hgs[k][0], jnp.bitwise_xor(me_ref[0], k), early * G)
    for b in range(2):
        hg = grad[b].reshape(block, width)
        rows = slice(b * block, (b + 1) * block)
        dx_ref[0, rows, :] = _dot(ft[b], hg).astype(BF16)
        acc[b] += _dot_nt(hg, x_ref[0, rows, :])

    @pl.when(c == pl.num_programs(1) - 1)
    def _():
        share = block // ndp
        for slot in range(ndp):
            start = pl.multiple_of(jnp.bitwise_xor(me_ref[1], slot) * share, share)
            part = acc[:, pl.ds(start, share), :] * factor
            to = sent if slot % 2 else kept
            to[slot // 2] = part.astype(to.dtype)


def block_grads(me, f, x, hg, hgs, after, nseq, ndp, factor, cb):
    lb, block, _ = f.shape
    width = x.shape[2]
    share = block // ndp
    lo = block // nseq
    rows = pl.BlockSpec((1, 2 * block, cb), lambda b, c, m: (0, b, c))
    return _call(
        functools.partial(block_grads_kernel, nseq, ndp, lo, factor),
        (lb // 2, width // cb),
        [
            pl.BlockSpec((2, block, block), lambda b, c, m: (b, 0, 0)),
            rows,
            pl.BlockSpec((nseq, 1, hg.shape[2], T, cb), lambda b, c, m: (0, b, 0, 0, c)),
        ]
        + [pl.BlockSpec((1, hgs[0].shape[1], T, cb), lambda b, c, m: (b, 0, 0, c))] * nseq,
        [rows] + [pl.BlockSpec((ndp // 2, 2, share, block), lambda b, c, m: (0, b, 0, 0))] * 2,
        [
            jax.ShapeDtypeStruct(x.shape, BF16),
            jax.ShapeDtypeStruct((ndp // 2, lb, share, block), F32),
            jax.ShapeDtypeStruct((ndp // 2, lb, share, block), BF16),
        ],
        [
            pltpu.VMEM((2, block, block), BF16),
            pltpu.VMEM((2, nseq, lo, cb), BF16),
            pltpu.VMEM((2, block, block), F32),
        ],
        4 * lb * block * block * width,
        6 * lb * block * width,
        "block_grads",
        after,
    )(me, f, x, hg, *[hgs[k] for k in [0] + _wire_order(nseq)], *after)


def mixed_kernel(nseq, ndp, lb, nb, factor, me_ref, s_ref, gate_ref, cot_ref, *rest):
    hs = dict(zip([0] + _wire_order(nseq), rest[:nseq]))
    gg_ref, out, pick, mask, flat, order, choose, m, hid, mg = rest[-10:]
    rows, cols = nb * G, G * nb
    share = nb // ndp
    width = gg_ref.shape[2]

    @pl.when(pl.program_id(0) == 0)
    def _():
        pick[...] = _pick(nb, lb, me_ref[0])
        same = _iota((cols, rows), 1) % G == _iota((cols, rows), 0) // nb
        mask[...] = same.astype(F32)
        same = _iota((rows, cols), 0) % G == _iota((rows, cols), 1) // nb
        flat[...] = same.astype(F32) * factor
        r = _iota((nb, nb), 1)
        block = jnp.bitwise_xor(r // lb, me_ref[0]) * lb + r % lb
        order[...] = (block == _iota((nb, nb), 0)).astype(BF16)
        q = _iota((cols, cols), 1)
        choose[...] = (_iota((cols, cols), 0) == (q % G) * nb + q // G).astype(BF16)

    m[...] = (_dot_nt(s_ref[...], pick[...]) * mask[...]).astype(BF16)
    for k in range(nseq):
        hid[k * lb * G:(k + 1) * lb * G, :] = hs[k][...].reshape(lb * G, width)
    for c in range(0, width, 256):
        cot = cot_ref[0, :, c:c + 256]
        mixed = _dot(m[...], hid[:, c:c + 256])
        gg_ref[0, :, c:c + 256] = (cot.astype(F32) * mixed).astype(BF16)
        mg[:, c:c + 256] = cot * gate_ref[0, :, c:c + 256]
    kept = _dot_nt(hid[...], mg[...]) * flat[...]
    terms = jnp.sum(kept.reshape(nb, G, cols), axis=1)
    terms = _dot(order[...], terms.astype(BF16)).astype(BF16)
    terms = _dot(terms, choose[...])
    tall = out.shape[2]
    for z in range(ndp):
        part = terms[:, z * share * G:(z + 1) * share * G]
        part = [part[r:r + tall] for r in range(0, nb, tall)]
        out[z, 0] = jnp.concatenate(part, axis=1).astype(BF16)


def mixed_stage(me, s2, gate, cot, hs, prev, after, g0, ng, groups, nseq, ndp, lb, nb, factor):
    width = gate.shape[2]
    rows = pl.BlockSpec((1, G * nb, width), lambda g, m: (0, g0 + g, 0))
    share = nb // ndp
    extra = list(prev) + list(after)
    square = (G * nb, nb * G)
    wide = max(128, share * G)
    tall = nb * share * G // wide
    return _call(
        functools.partial(mixed_kernel, nseq, ndp, lb, nb, factor),
        (ng,),
        [pl.BlockSpec((G * nb, nb), lambda g, m: (g0 + g, 0)), rows, rows]
        + [pl.BlockSpec((lb // 2, 1, T, width), lambda g, m: (0, g, 0, 0))] * nseq,
        [rows, pl.BlockSpec((ndp, 1, tall, wide), lambda g, m: (0, g0 + g, 0, 0))],
        [
            jax.ShapeDtypeStruct(gate.shape, BF16),
            jax.ShapeDtypeStruct((ndp, groups, tall, wide), BF16),
        ],
        [
            pltpu.VMEM((nb * G, nb), BF16),
            pltpu.VMEM(square, F32),
            pltpu.VMEM(square, F32),
            pltpu.VMEM((nb, nb), BF16),
            pltpu.VMEM((G * nb, G * nb), BF16),
            pltpu.VMEM(square, BF16),
            pltpu.VMEM((nb * G, width), BF16),
            pltpu.VMEM((G * nb, width), BF16),
        ],
        4 * ng * (G * nb) ** 2 * width,
        8 * ng * G * nb * width,
        "mixed",
        extra,
        {4 + nseq + i: i for i in range(len(prev))},
    )(me, s2, gate, cot, *[hs[k] for k in [0] + _wire_order(nseq)], *extra)


def _wire_order(size):
    ks = list(range(2, size))
    last = [k for k in ks if k % 2]
    return [k for k in ks if k % 2 == 0][::-1] + last[::-1] + [1]


def _swap(parts, axis, size, differences):
    got = dict([(0, parts[0])])
    for k in differences:
        got[k] = lax.ppermute(parts[k], axis, [(s, s ^ k) for s in range(size)])
    return got


def _pass(part, axis, size, step):
    return lax.ppermute(part, axis, [(z, z ^ step) for z in range(size)])


def _halve(kept, got, axis, size):
    step = 2
    while step < size:
        kept = kept + got.astype(F32)
        got = _pass(kept[1::2].astype(BF16), axis, size, step)
        kept = kept[0::2]
        step *= 2
    return kept, got


def _behind(parts, ahead, count):
    first = _wire_order(len(ahead))[:count]
    parts, arrived = lax.optimization_barrier((parts, [ahead[k] for k in first]))
    for k, part in zip(first, arrived):
        ahead[k] = part
    return parts


def _exchange(parts, axis):
    return lax.all_to_all(parts, axis, split_axis=0, concat_axis=0, tiled=True)


def _total(parts):
    return jnp.sum(parts.astype(F32), axis=0)


def local(tokens, gate, cotangent, first_factor, second_factor):
    seqs, _, width = tokens.shape
    ndp, nseq = lax.axis_size("dp"), lax.axis_size("seq")
    lb = first_factor.shape[0]
    lo, nb = second_factor.shape[:2]
    groups = lo // G
    early = groups // 4 if groups >= 8 else groups // 2
    late = early
    factor = 1.0 / float(width * seqs * ndp) ** 0.5
    me = jnp.stack([lax.axis_index("seq"), lax.axis_index("dp")]).astype(jnp.int32)

    s2_early = second_factor[:early * G].reshape(early * G * nb, nb)
    still = np.array([0, 1], np.int32)
    back_a = hidden_grad(still, s2_early, gate, cotangent, (), 0, early, False, nseq, lb, nb)
    second_factor, back_a = lax.optimization_barrier((second_factor, back_a))
    s2 = second_factor.reshape(lo * nb, nb)
    grad_a = lax.all_to_all(back_a, "seq", split_axis=0, concat_axis=0, tiled=True)
    back_b = hidden_grad(
        me, s2, gate, cotangent, (back_a,), early, groups - early, True, nseq, lb, nb
    )
    spans = ((0, groups - late), (groups - late, late))
    hidden_b, hidden_c = hidden_forward(
        me, first_factor, tokens, (back_b[0],), spans, nseq, lo, 1024
    )
    back_b, grad_a, hidden_b = lax.optimization_barrier((back_b, grad_a, hidden_b))
    grad_b = _swap(back_b, "seq", nseq, _wire_order(nseq))
    wire = _wire_order(nseq)
    got_b = _swap(_behind(hidden_b, grad_b, nseq - 3), "seq", nseq, wire)
    hidden_c = _behind(hidden_c, got_b, 3)
    got_c = _swap(hidden_c, "seq", nseq, wire[:-1])
    input_grad, kept, sent = block_grads(
        me, first_factor, tokens, grad_a, grad_b, (), nseq, ndp, factor, 1024
    )
    sent = _behind(sent, got_b, 2)

    halves = _pass(sent, "dp", ndp, 1)

    gate_grad, terms = mixed_stage(
        me, s2, gate, cotangent, got_b, (), (sent,), 0, groups - late, groups,
        nseq, ndp, lb, nb, factor
    )
    last_c, terms = lax.optimization_barrier((hidden_c[wire[-1]], terms))
    hidden_c[wire[-1]] = last_c
    got_c.update(_swap(hidden_c, "seq", nseq, wire[-1:]))
    kept, first_got = _halve(kept, halves, "dp", ndp)
    gate_grad, terms = mixed_stage(
        me, s2, gate, cotangent, got_c, (gate_grad, terms), (), groups - late, late, groups,
        nseq, ndp, lb, nb, factor
    )
    share = nb // ndp
    terms, first_got = lax.optimization_barrier((terms, first_got))
    first_share = (kept + first_got.astype(F32))[0]
    second_share = _total(_exchange(terms, "dp")).reshape(groups, terms.shape[2], -1, share, G)
    second_share = second_share.transpose(0, 4, 3, 2, 1).reshape(lo, share, nb)
    return (input_grad, gate_grad, first_share, second_share)


def solution(mesh):
    placed = (
        P("dp", "seq", None),
        P("dp", "seq", None),
        P("dp", "seq", None),
        P("seq", None, None),
        P("seq", None, None),
    )
    return jax.shard_map(
        local,
        mesh=mesh,
        in_specs=placed,
        out_specs=(
            P("dp", "seq", None),
            P("dp", "seq", None),
            P("seq", "dp", None),
            P("seq", "dp", None),
        ),
        check_vma=False,
    )
```
